32 devices in a mesh: groups: 2 (over x), row: 16 (over z, y, core).
Axes of the slice: x: 2, y: 2, z: 4, core: 2. Of those that a mesh axis runs over, the one named last changes fastest.
Arguments:
- inverse: float32 [4, 4096, 4096], P('groups', 'row'), parts along dimension 0, as said below
- cycle: bfloat16 [4, 4096, 1024], P('groups', 'row'), parts along dimension 0, as said below
- arrivals: bfloat16 [4, 2, 4096, 128], P('groups', None, 'row'), parts along dimension 0, may hold values from -6 to 6
- departing: int32 [4, 128], P('groups'), parts along dimension 0, may hold values from 0 to 1023, as said below
- directions: int32 [4, 512], P('groups'), parts along dimension 0, may hold values from 0 to 8191
Outputs:
- new_inverse: float32 [4, 4096, 4096], P('groups', 'row'), parts along dimension 0
- beam_weights: float32 [4, 2, 4096, 512], P('groups', None, 'row'), parts along dimension 0
- spectrum: float32 [4, 512], P('groups'), parts along dimension 0
The draws below stay inside these ranges and needn't reach their ends.
There are 2 independent parts, one for each index of `groups`. The reference program is written for one: setup_inputs(seed, part) draws one part's arguments, and reference() takes and returns one part's arrays. A program takes and returns all parts, laid end to end along the dimension named above; each array names one. Nothing has to cross between parts.
Inputs may be any that keep to these rules, and one draw needn't show every extreme that they name: inverse is Hermitian and is the inverse of I + cycle cycle^H / 1024. `cycle`: the snapshots whose inverse covariance is given. `departing`: all 2 x 128 entries are different slots.
All inputs are finite; a program needn't handle non-finite values.
Results may differ from the reference program's by a relative error of at most 0.0003.
Values may be sent and summed in bfloat16 or wider, within the bound.
A program may use at most 192 MiB of HBM per device.

```python
import jax
import jax.numpy as jnp
from jax import lax

M = 4096
SNAP = 128
CYCLE = 1024
STEPS = 2
DIRS = 512
ANGLES = 8192


def window_snapshots(key):
    base = jax.random.fold_in(key, 7)
    values = jax.random.normal(base, (2, M, CYCLE), jnp.float32)
    return values.astype(jnp.bfloat16)


def draw_cycle(key, part):
    return window_snapshots(key)


def draw_inverse(key, part):
    snaps = window_snapshots(key).astype(jnp.float32)
    snap_re, snap_im = (snaps[0], snaps[1])
    hp = lax.Precision.HIGHEST
    gram_re = jnp.dot(snap_re.T, snap_re, precision=hp) + jnp.dot(snap_im.T, snap_im, precision=hp)
    gram_im = jnp.dot(snap_re.T, snap_im, precision=hp) - jnp.dot(snap_im.T, snap_re, precision=hp)
    gram_re = gram_re + CYCLE * jnp.eye(CYCLE, dtype=jnp.float32)
    embedded = jnp.concatenate([jnp.concatenate([gram_re, -gram_im], 1), jnp.concatenate([gram_im, gram_re], 1)], 0)
    rhs = jnp.concatenate([snap_re.T, -snap_im.T], 0)
    solution = jnp.linalg.solve(embedded, rhs)
    sol_re, sol_im = (solution[:CYCLE], solution[CYCLE:])
    prod_re = jnp.dot(snap_re, sol_re, precision=hp) - jnp.dot(snap_im, sol_im, precision=hp)
    prod_im = jnp.dot(snap_re, sol_im, precision=hp) + jnp.dot(snap_im, sol_re, precision=hp)
    inv_re = jnp.eye(M, dtype=jnp.float32) - prod_re
    inv_im = -prod_im
    inv_re = 0.5 * (inv_re + inv_re.T)
    inv_im = 0.5 * (inv_im - inv_im.T)
    return jnp.stack([inv_re, inv_im]).astype(jnp.float32)


def draw_departing(key, part):
    total = STEPS * SNAP
    others = jax.random.permutation(jax.random.fold_in(key, 11), CYCLE - 1)[:total - 1]
    chosen = jnp.concatenate([others.astype(jnp.int32), jnp.full((1,), CYCLE - 1, jnp.int32)])
    mixed = jax.random.permutation(jax.random.fold_in(key, 13), chosen)
    return mixed.reshape(STEPS, SNAP).astype(jnp.int32)


def set_ends(entries, key, smallest, top_value):
    spot = [jax.random.randint(jax.random.fold_in(key, axis), (), 0, length) for axis, length in enumerate(entries.shape)]
    main_axis = entries.shape.index(max(entries.shape))
    neighbour = spot[:main_axis] + [(spot[main_axis] + 1) % entries.shape[main_axis]] + spot[main_axis + 1:]
    return entries.at[tuple(spot)].set(smallest).at[tuple(neighbour)].set(top_value)


def shard_levels(rng, dims, pieces, low, high):
    def one(axis_at, shards_of):
        draws = jax.random.uniform(jax.random.fold_in(jax.random.fold_in(rng, 6), axis_at), (shards_of,), jnp.float32, low / len(pieces), high / len(pieces))
        return jnp.repeat(jnp.exp(draws), dims[axis_at] // shards_of).reshape((-1,) + (1,) * (len(dims) - axis_at - 1))

    gain = one(*pieces[0])
    for cut in pieces[1:]:
        gain = gain * one(*cut)
    return gain


def noise(rng, extent, deviation, most, split=(), kind=jnp.bfloat16):
    result = deviation * jax.random.normal(rng, extent, jnp.float32)
    if split:
        result = result * shard_levels(rng, extent, split, -0.22, 0.18)
    return jnp.clip(result, -most, most).astype(kind)


def setup_inputs(seed: int = 0, part: int = 0) -> dict:
    key_list = jax.random.split(jax.random.key(seed), 6)
    part_keys = jax.random.split(jax.random.fold_in(key_list[5], part), 6)
    return {
        "inverse": draw_inverse(jax.random.fold_in(jax.random.fold_in(key_list[5], part), 71), part),
        "cycle": draw_cycle(jax.random.fold_in(jax.random.fold_in(key_list[5], part), 71), part),
        "arrivals": noise(part_keys[2], (STEPS, 2, M, SNAP), 1.0, 6.0, ((2, 16),)),
        "departing": draw_departing(jax.random.fold_in(jax.random.fold_in(key_list[5], part), 71), part),
        "directions": set_ends(jax.random.randint(part_keys[4], (STEPS, DIRS), 0, ANGLES), jax.random.fold_in(part_keys[4], 1), 0, ANGLES - 1).astype(jnp.int32),
    }


precise = lax.Precision.HIGHEST

def matmul(left, right):
    return jnp.dot(left.astype(jnp.float32), right.astype(jnp.float32), precision=precise, preferred_element_type=jnp.float32)

def lead_dot(left, right):
    return lax.dot_general(left.astype(jnp.float32), right.astype(jnp.float32), (((0,), (0,)), ((), ())), precision=precise, preferred_element_type=jnp.float32)

def steering(direction_ids, length):
    element = jnp.arange(length, dtype=jnp.int32)[:, None]
    odd_index = 2 * direction_ids[None, :] + 1
    angle_count = 2 * length
    turns = (element * odd_index - element * angle_count) % (2 * angle_count)
    phase = jnp.pi * turns.astype(jnp.float32) / angle_count
    return (jnp.cos(phase), jnp.sin(phase))

def reference(inverse, cycle, arrivals, departing, directions):
    inv_re, inv_im = (inverse[0], inverse[1])
    weight_list = []
    power_list = []
    for step_index in range(STEPS):
        steer_re, steer_im = steering(directions[step_index], M)
        app_re = matmul(inv_re, steer_re) - matmul(inv_im, steer_im)
        app_im = matmul(inv_re, steer_im) + matmul(inv_im, steer_re)
        power = jnp.sum(steer_re * app_re + steer_im * app_im, axis=0)
        weight_list.append(jnp.stack([M * app_re / power, M * app_im / power]))
        power_list.append(M / power)
        departed = jnp.take(cycle, departing[step_index], axis=2)
        snap_wide = jnp.concatenate([arrivals[step_index], departed], axis=2).astype(jnp.float32)
        q_re = matmul(inv_re, snap_wide[0]) - matmul(inv_im, snap_wide[1])
        q_im = matmul(inv_re, snap_wide[1]) + matmul(inv_im, snap_wide[0])
        cap_re = lead_dot(snap_wide[0], q_re) + lead_dot(snap_wide[1], q_im)
        cap_im = lead_dot(snap_wide[0], q_im) - lead_dot(snap_wide[1], q_re)
        signs = jnp.concatenate([jnp.ones((SNAP,), jnp.float32), -jnp.ones((SNAP,), jnp.float32)])
        g_re = CYCLE * jnp.diag(signs) + cap_re
        g_im = cap_im
        embedded = jnp.concatenate([jnp.concatenate([g_re, -g_im], 1), jnp.concatenate([g_im, g_re], 1)], 0)
        rhs = jnp.concatenate([q_re.T, -q_im.T], 0)
        solution = jnp.linalg.solve(embedded, rhs)
        half = 2 * SNAP
        x_re, x_im = (solution[:half], solution[half:])
        inv_re = inv_re - (matmul(q_re, x_re) - matmul(q_im, x_im))
        inv_im = inv_im - (matmul(q_re, x_im) + matmul(q_im, x_re))
    return (jnp.stack([inv_re, inv_im]), jnp.stack(weight_list), jnp.stack(power_list))
```

```python
import functools

import jax
import jax.numpy as jnp
from jax import lax
from jax.experimental import pallas as pl
from jax.experimental.pallas import tpu as pltpu
from jax.sharding import PartitionSpec as P

f32, bf16 = jnp.float32, jnp.bfloat16
HIGHEST = lax.Precision.HIGHEST
VMEM_LIMIT = 56 * 2**20
FINE = 16


def halves(x):
    top = x.astype(bf16)
    return top, (x - top.astype(f32)).astype(bf16)


def dot1(left, right, dims=((1,), (0,))):
    return lax.dot_general(left, right, (dims, ((), ())), preferred_element_type=f32)


def dot3(left, right, dims=((1,), (0,))):
    lt, lb = halves(left)
    rt, rb = halves(right)
    return dot1(lt, rt, dims) + dot1(lt, rb, dims) + dot1(lb, rt, dims)


def dot6(left, right, dims=((1,), (0,))):
    return lax.dot_general(left, right, (dims, ((), ())), precision=HIGHEST, preferred_element_type=f32)


def cis(turns, half_turn):
    phase = jnp.pi * (turns % (2 * half_turn)).astype(f32) / half_turn
    return jnp.cos(phase), jnp.sin(phase)


def steer_kernel(blocks, low_ref, high_ref, coarse_ref, fine_ref, turn_ref, out_ref, acc, rhs_t, rhs_b):
    step = pl.program_id(0)
    rows, width = low_ref.shape[1:]
    coarse = width // FINE

    row = lax.broadcasted_iota(jnp.int32, (width, width), 0)
    col = lax.broadcasted_iota(jnp.int32, (width, width), 1)
    flip = (row + col == width - 1).astype(bf16)
    low_t, low_b = halves(jnp.concatenate([low_ref[0], low_ref[1]], 0))
    low = dot1(low_t, flip) + dot1(low_b, flip)
    high = jnp.concatenate([high_ref[0], high_ref[1]], 0)
    total, diff = high + low, high - low
    left = jnp.concatenate([total, jnp.concatenate([-diff[rows:], diff[:rows]], 0)], 1)
    left_t, left_b = halves(left)

    fine_c, fine_s = fine_ref[0], fine_ref[1]
    for q in range(coarse):
        cc, cs = coarse_ref[0, q : q + 1, :], coarse_ref[1, q : q + 1, :]
        for part, value in enumerate((cc * fine_c - cs * fine_s, cs * fine_c + cc * fine_s)):
            top, rest = halves(value)
            place = pl.ds(part * width + q * FINE, FINE)
            rhs_t[place, :] = top
            rhs_b[place, :] = rest
    top = rhs_t[...]
    term = dot1(left_t, top) + dot1(left_t, rhs_b[...]) + dot1(left_b, top)

    @pl.when(step == 0)
    def _():
        acc[...] = term

    @pl.when(step > 0)
    def _():
        acc[...] += term

    @pl.when(step == blocks - 1)
    def _():
        turn_c, turn_s = turn_ref[0:1, :], turn_ref[1:2, :]
        re, im = acc[:rows, :], acc[rows:, :]
        out_ref[0] = re * turn_c - im * turn_s
        out_ref[1] = re * turn_s + im * turn_c


def steer_product(inverse, odd):
    _, rows, length = inverse.shape
    cols = odd.shape[0]
    width = min(256, length // 2)
    blocks = length // 2 // width
    half_turn = 4 * length
    coarse = jnp.stack(cis(2 * FINE * jnp.arange(length // 2 // FINE, dtype=jnp.int32)[:, None] * odd[None, :], half_turn))
    fine = jnp.stack(cis((2 * jnp.arange(FINE, dtype=jnp.int32)[:, None] + 1) * odd[None, :], half_turn))
    turn = jnp.stack(cis((length - 1) * odd, half_turn))
    return pl.pallas_call(
        functools.partial(steer_kernel, blocks),
        grid=(blocks,),
        in_specs=[
            pl.BlockSpec((2, rows, width), lambda i: (0, 0, blocks - 1 - i)),
            pl.BlockSpec((2, rows, width), lambda i: (0, 0, blocks + i)),
            pl.BlockSpec((2, width // FINE, cols), lambda i: (0, i, 0)),
            pl.BlockSpec((2, FINE, cols), lambda i: (0, 0, 0)),
            pl.BlockSpec((2, cols), lambda i: (0, 0)),
        ],
        out_specs=pl.BlockSpec((2, rows, cols), lambda i: (0, 0, 0)),
        out_shape=jax.ShapeDtypeStruct((2, rows, cols), f32),
        scratch_shapes=[
            pltpu.VMEM((2 * rows, cols), f32),
            pltpu.VMEM((2 * width, cols), bf16),
            pltpu.VMEM((2 * width, cols), bf16),
        ],
        compiler_params=pltpu.CompilerParams(vmem_limit_bytes=VMEM_LIMIT),
        cost_estimate=pl.CostEstimate(
            flops=3 * 2 * 2 * rows * length * cols, bytes_accessed=8 * rows * length, transcendentals=0
        ),
    )(inverse, inverse, coarse, fine, turn)


def definite_inverse(matrix):
    size = matrix.shape[0]
    row = lax.broadcasted_iota(jnp.int32, (size, size), 0)
    col = lax.broadcasted_iota(jnp.int32, (size, size), 1)
    eye = (row == col).astype(f32)
    scale_c = lax.rsqrt(jnp.sum(matrix * eye, axis=1, keepdims=True))
    scale_r = lax.rsqrt(jnp.sum(matrix * eye, axis=0, keepdims=True))
    unit = matrix * scale_c * scale_r
    bound = jnp.max(jnp.sum(jnp.abs(unit), axis=0, keepdims=True))
    start = eye * (1.0 / bound)
    unit_t = unit.astype(bf16)

    def square(x):
        return jnp.sum(x * x)

    def rough_next(state):
        guess, _, last, count = state
        guess_t = guess.astype(bf16)
        residual = eye - dot1(unit_t, guess_t)
        return guess + dot1(guess_t, residual.astype(bf16)), last, square(residual), count + 1

    def rough_more(state):
        _, before, last, count = state
        return (last > 0.05) & (last < before) & (count < 16)

    big = jnp.float32(1e30)
    rough = lax.while_loop(rough_more, rough_next, (start, big * 2, big, jnp.int32(0)))[0]
    first = square(eye - dot6(unit, rough))
    guess = jnp.where(first < 0.9, rough, start)

    def fine_next(state):
        guess, _, last, count = state
        residual = eye - dot6(unit, guess)
        return guess + dot6(guess, residual), last, square(residual), count + 1

    def fine_more(state):
        _, before, last, count = state
        stalled = (last < 0.25) & (last > 0.5 * before)
        return (last > 1e-6) & jnp.logical_not(stalled) & (count < 50)

    guess = lax.while_loop(fine_more, fine_next, (guess, big * 2, big, jnp.int32(0)))[0]
    return guess * scale_c * scale_r


def finish_kernel(steps, window, length, cap_ref, cross_ref, q_ref, applied_ref, fold_ref, weights_ref, spectrum_ref, work, left):
    count = 2 * steps
    snap = cap_ref.shape[1] // count
    size = 2 * snap
    rows = q_ref.shape[1]
    lead = 2 * snap
    dirs = cross_ref.shape[2]
    eye = (
        lax.broadcasted_iota(jnp.int32, (snap, snap), 0) == lax.broadcasted_iota(jnp.int32, (snap, snap), 1)
    ).astype(f32) * window
    for i in range(count):
        up, mid, down = i * size, i * size + snap, (i + 1) * size
        for j in range(count):
            at, half, end = j * size, j * size + snap, (j + 1) * size
            re = cap_ref[0, i * snap : (i + 1) * snap, j * snap : (j + 1) * snap]
            im = cap_ref[1, i * snap : (i + 1) * snap, j * snap : (j + 1) * snap]
            if i == j:
                re = re + (eye if i % 2 == 0 else -eye)
            work[up:mid, at:half] = re
            work[up:mid, half:end] = -im
            work[mid:down, at:half] = im
            work[mid:down, half:end] = re
        re = q_ref[0, :, i * snap : (i + 1) * snap]
        im = q_ref[1, :, i * snap : (i + 1) * snap]
        left[:rows, up:mid] = re
        left[:rows, mid:down] = -im
        if i < 2:
            left[rows:, up:mid] = im
            left[rows:, mid:down] = re

    def body(k, carry):
        sign = jnp.where(k % 2 == 0, 1.0, -1.0)
        here = pl.ds(pl.multiple_of(k * size, size), size)
        pivot = definite_inverse(sign * work[here, here]) * sign
        across = dot6(pivot, work[here, :])
        work[here, :] = across
        work[here, here] = pivot

        def other(step, carry):
            i = lax.rem(k + step, count)
            there = pl.ds(pl.multiple_of(i * size, size), size)
            column = work[there, here]
            work[there, here] = jnp.zeros_like(column)
            work[there, :] -= dot6(column, work[here, :])
            return carry

        lax.fori_loop(1, count, other, 0)

        @pl.when(k == 1)
        def _():
            stacked = jnp.concatenate(
                [cross_ref[p, i * snap : (i + 1) * snap] for i in range(2) for p in range(2)], 0
            )
            solved = dot3(work[: 2 * size, : 2 * size], stacked)
            drop = jnp.sum(stacked * solved, axis=0, keepdims=True)
            moved = dot3(left[:, : 2 * size], solved)
            first = cross_ref[0, lead : lead + 1]
            second = cross_ref[1, lead : lead + 1] - drop
            first, second = length / first, length / second
            spectrum_ref[0:1] = first
            spectrum_ref[1:2] = second
            for p in range(2):
                weights_ref[0, p] = applied_ref[p, :, :dirs] * first
                weights_ref[1, p] = (applied_ref[p, :, dirs:] - moved[p * rows : (p + 1) * rows]) * second

        return carry

    lax.fori_loop(0, count, body, 0)
    fold = dot3(left[:rows], work[...])
    for i in range(count):
        fold_ref[0, :, i * snap : (i + 1) * snap] = fold[:, i * size : i * size + snap]
        fold_ref[1, :, i * snap : (i + 1) * snap] = -fold[:, i * size + snap : (i + 1) * size]


def finish(cap, cross, q, applied, steps, window, length):
    order = cap.shape[1]
    rows = q.shape[1]
    dirs = cross.shape[2]
    return pl.pallas_call(
        functools.partial(finish_kernel, steps, window, length),
        in_specs=[pl.BlockSpec(memory_space=pltpu.VMEM)] * 4,
        out_specs=[pl.BlockSpec(memory_space=pltpu.VMEM)] * 3,
        out_shape=[
            jax.ShapeDtypeStruct((2, rows, order), f32),
            jax.ShapeDtypeStruct((steps, 2, rows, dirs), f32),
            jax.ShapeDtypeStruct((steps, dirs), f32),
        ],
        scratch_shapes=[pltpu.VMEM((2 * order, 2 * order), f32), pltpu.VMEM((2 * rows, 2 * order), f32)],
        compiler_params=pltpu.CompilerParams(vmem_limit_bytes=VMEM_LIMIT),
        cost_estimate=pl.CostEstimate(flops=50 * 10**9, bytes_accessed=10**7, transcendentals=0),
    )(cap, cross, q, applied)


def update_kernel(inv_ref, fold_ref, part_ref, scale_ref, out_ref):
    rows = inv_ref.shape[1]
    scale = scale_ref[0]
    fold_re = jnp.concatenate([fold_ref[0] * scale[0:1, :], fold_ref[1] * scale[1:2, :]], 1)
    fold_im = jnp.concatenate([fold_ref[1] * scale[0:1, :], -fold_ref[0] * scale[1:2, :]], 1)
    top, rest = halves(jnp.concatenate([fold_re, fold_im], 0))
    both = part_ref[...]
    low = (both << 16) >> 16
    value = jnp.concatenate([(both - low) >> 16, low], 1)
    upper = (value + 128) >> 8
    lower = (value - upper * 256).astype(f32).astype(bf16)
    upper = (upper * 256).astype(f32).astype(bf16)
    dims = ((1,), (1,))
    change = dot1(top, upper, dims) + dot1(rest, upper, dims) + dot1(top, lower, dims)
    out_ref[0] = inv_ref[0] - change[:rows]
    out_ref[1] = inv_ref[1] - change[rows:]


def low_rank_update(inverse, fold, parts, scales):
    _, rows, length = inverse.shape
    order = fold.shape[2]
    return pl.pallas_call(
        update_kernel,
        grid=(length // rows,),
        in_specs=[
            pl.BlockSpec((2, rows, rows), lambda i: (0, 0, i)),
            pl.BlockSpec((2, rows, order), lambda i: (0, 0, 0)),
            pl.BlockSpec((rows, order), lambda i: (i, 0)),
            pl.BlockSpec((1, 2, order), lambda i: (i, 0, 0)),
        ],
        out_specs=pl.BlockSpec((2, rows, rows), lambda i: (0, 0, i)),
        out_shape=jax.ShapeDtypeStruct(inverse.shape, f32),
        compiler_params=pltpu.CompilerParams(vmem_limit_bytes=VMEM_LIMIT),
        cost_estimate=pl.CostEstimate(
            flops=24 * rows * order * length, bytes_accessed=16 * rows * length, transcendentals=0
        ),
    )(inverse, fold, parts, scales)


def product_kernel(blocks, lead, inv_ref, all_ref, snaps_ref, applied_ref, coarse_ref, fine_ref,
                   q_ref, cap_ref, cross_ref, parts_ref, scale_ref, acc, steer):
    step = pl.program_id(0)
    rows = inv_ref.shape[1]
    order = snaps_ref.shape[2]
    left = jnp.concatenate(halves(jnp.concatenate([inv_ref[0], inv_ref[1]], 0)), 0)
    term = dot1(left, jnp.concatenate([all_ref[0], all_ref[1]], 1))

    @pl.when(step == 0)
    def _():
        acc[...] = term

    @pl.when(step > 0)
    def _():
        acc[...] += term

    @pl.when(step == blocks - 1)
    def _():
        total = acc[: 2 * rows] + acc[2 * rows :]
        re = total[:rows, :order] - total[rows:, order:]
        im = total[:rows, order:] + total[rows:, :order]
        q_ref[0] = re
        q_ref[1] = im
        packed = 0
        for part, value in enumerate((re, im)):
            peak = jnp.max(jnp.abs(value), axis=0, keepdims=True)
            scale = jnp.where(peak > 0, peak, 1.0) / 32767.0
            scale_ref[0, part : part + 1] = scale
            whole = jnp.clip(jnp.round(value / scale), -32767, 32767).astype(jnp.int32)
            packed = packed * 65536 + whole
        parts_ref[...] = packed

        dims = ((0,), (0,))
        both = jnp.concatenate([re, im], 1)
        snaps = jnp.concatenate([snaps_ref[0], snaps_ref[1]], 1)
        top = both.astype(bf16)
        mid, low = halves(both - top.astype(f32))
        sums = dot1(snaps, top, dims) + dot1(snaps, mid, dims) + dot1(snaps, low, dims)
        cap_ref[0] = sums[:order, :order] + sums[order:, order:]
        cap_ref[1] = sums[:order, order:] - sums[order:, :order]

        cols = steer.shape[2]
        dirs = cols // 2
        fine_c, fine_s = fine_ref[0], fine_ref[1]
        for g in range(rows // FINE):
            cc, cs = coarse_ref[0, g : g + 1, :], coarse_ref[1, g : g + 1, :]
            steer[0, g * FINE : (g + 1) * FINE, :] = cc * fine_c - cs * fine_s
            steer[1, g * FINE : (g + 1) * FINE, :] = cs * fine_c + cc * fine_s
        power = jnp.sum(steer[0] * applied_ref[0] + steer[1] * applied_ref[1], axis=0, keepdims=True)
        first = jnp.concatenate([re[:, :lead], im[:, :lead]], 1)
        later = jnp.concatenate([steer[0, :, dirs:], steer[1, :, dirs:]], 1)
        sums = dot3(first, later, dims)
        cross_ref[0, :lead] = sums[:lead, :dirs] + sums[lead:, dirs:]
        cross_ref[1, :lead] = sums[:lead, dirs:] - sums[lead:, :dirs]
        extra = cross_ref.shape[1] - lead
        cross_ref[0, lead:] = jnp.broadcast_to(power[:, :dirs], (extra, dirs))
        cross_ref[1, lead:] = jnp.broadcast_to(power[:, dirs:], (extra, dirs))


def product(inverse, snaps_all, snaps, applied, coarse, fine, lead):
    _, rows, length = inverse.shape
    order = snaps.shape[2]
    cols = applied.shape[2]
    width = min(512, length)
    blocks = length // width
    keep = lambda *shape: pl.BlockSpec(shape, lambda i: (0,) * len(shape))
    shapes = [
        ((2, rows, order), f32),
        ((2, order, order), f32),
        ((2, lead + 8, cols // 2), f32),
        ((rows, order), jnp.int32),
        ((1, 2, order), f32),
    ]
    return pl.pallas_call(
        functools.partial(product_kernel, blocks, lead),
        grid=(blocks,),
        in_specs=[
            pl.BlockSpec((2, rows, width), lambda i: (0, 0, i)),
            pl.BlockSpec((2, width, order), lambda i: (0, i, 0)),
            keep(*snaps.shape),
            keep(*applied.shape),
            keep(*coarse.shape),
            keep(*fine.shape),
        ],
        out_specs=[keep(*shape) for shape, _ in shapes],
        out_shape=[jax.ShapeDtypeStruct(shape, kind) for shape, kind in shapes],
        scratch_shapes=[pltpu.VMEM((4 * rows, 2 * order), f32), pltpu.VMEM((2, rows, cols), f32)],
        compiler_params=pltpu.CompilerParams(vmem_limit_bytes=VMEM_LIMIT),
        cost_estimate=pl.CostEstimate(
            flops=16 * rows * length * order, bytes_accessed=16 * rows * length, transcendentals=0
        ),
    )(inverse, snaps_all, snaps, applied, coarse, fine)


def on_device(inverse, cycle, arrivals, departing, directions):
    _, rows, length = inverse.shape
    window = cycle.shape[2]
    steps, _, _, snap = arrivals.shape
    dirs = directions.shape[1]

    slots = lax.broadcasted_iota(jnp.int32, (window, steps * snap), 0)
    pick = (slots == departing.reshape(1, -1)).astype(bf16)
    departed = dot1(cycle.reshape(2 * rows, window), pick).astype(bf16).reshape(2, rows, steps, snap)
    snaps = jnp.concatenate([jnp.moveaxis(arrivals, 0, 2), departed], axis=3).reshape(2, rows, 2 * steps * snap)
    snaps_all = lax.all_gather(snaps, "row", axis=1, tiled=True)

    odd = (2 * directions + 1 - 2 * length).reshape(-1)
    applied = steer_product(inverse, odd)

    first_row = lax.axis_index("row") * rows
    coarse = jnp.stack(
        cis((first_row + FINE * jnp.arange(rows // FINE, dtype=jnp.int32))[:, None] * odd[None, :], 2 * length)
    )
    fine = jnp.stack(cis(jnp.arange(FINE, dtype=jnp.int32)[:, None] * odd[None, :], 2 * length))
    q, cap, cross, parts, scale = product(inverse, snaps_all, snaps, applied, coarse, fine, 2 * snap)
    cap, cross = lax.psum((cap, cross), "row")
    parts_all = lax.all_gather(parts, "row", axis=0, tiled=True)
    scales_all = lax.all_gather(scale, "row", axis=0, tiled=True)

    fold, weights, spectrum = finish(cap, cross, q, applied, steps, window, length)
    new_inverse = low_rank_update(inverse, fold, parts_all, scales_all)
    return new_inverse, weights, spectrum


def solution(mesh):
    in_specs = (
        P("groups", "row", None),
        P("groups", "row", None),
        P("groups", None, "row", None),
        P("groups", None),
        P("groups", None),
    )
    out_specs = (P("groups", "row", None), P("groups", None, "row", None), P("groups", None))
    return jax.shard_map(
        on_device, mesh=mesh, in_specs=in_specs, out_specs=out_specs, check_vma=False
    )
```

```python
import functools

import jax
import jax.numpy as jnp
from jax import lax
from jax.experimental import pallas as pl
from jax.experimental.pallas import tpu as pltpu
from jax.sharding import PartitionSpec as P

f32, bf16 = jnp.float32, jnp.bfloat16
HIGHEST = lax.Precision.HIGHEST
VMEM_LIMIT = 56 * 2**20
FINE = 16


def halves(x):
    top = x.astype(bf16)
    return top, (x - top.astype(f32)).astype(bf16)


def dot1(left, right, dims=((1,), (0,))):
    return lax.dot_general(left, right, (dims, ((), ())), preferred_element_type=f32)


def dot3(left, right, dims=((1,), (0,))):
    lt, lb = halves(left)
    rt, rb = halves(right)
    return dot1(lt, rt, dims) + dot1(lt, rb, dims) + dot1(lb, rt, dims)


def dot6(left, right, dims=((1,), (0,))):
    return lax.dot_general(left, right, (dims, ((), ())), precision=HIGHEST, preferred_element_type=f32)


def cis(turns, half_turn):
    phase = jnp.pi * (turns % (2 * half_turn)).astype(f32) / half_turn
    return jnp.cos(phase), jnp.sin(phase)


TAIL = 16


def ring_place(chip, chips):
    odd = chip % 2
    return (1 - odd) * (chip // 2) + odd * (chips - 1 - chip // 2)


def ring_chip(place, chips):
    back = place // (chips // 2)
    return (1 - back) * 2 * place + back * (2 * (chips - place) - 1)


def gather_kernel(chips, x_ref, out_ref, own_sem, up_send, up_recv, down_send, down_recv, pair_send, pair_recv):
    me = lax.axis_index("row")
    core = me % 2
    place = ring_place(me // 2, chips)
    pair = me + 1 - 2 * core
    above = ring_chip((place + 1) % chips, chips) * 2 + core
    below = ring_chip((place + chips - 1) % chips, chips) * 2 + core
    mesh_id = pl.DeviceIdType.MESH
    half = x_ref.shape[0] // 2
    steps = chips // 2

    barrier = pltpu.get_barrier_semaphore()
    for device in (above, below, pair):
        pl.semaphore_signal(barrier, inc=1, device_id={"row": device}, device_id_type=mesh_id)
    pl.semaphore_wait(barrier, 3)

    def block(offset):
        return ring_chip((place + offset + chips) % chips, chips) * 2 + core

    def send(source, target, device, send_sem, recv_sem):
        copy = pltpu.make_async_remote_copy(
            src_ref=source, dst_ref=target, send_sem=send_sem, recv_sem=recv_sem,
            device_id={"row": device}, device_id_type=mesh_id,
        )
        copy.start()
        return copy

    own = pltpu.make_async_copy(x_ref, out_ref.at[me], own_sem)
    own.start()
    pairs = [send(x_ref, out_ref.at[me], pair, pair_send.at[0], pair_recv.at[0])]
    sent = []
    for t in range(steps):
        up, down = block(-t), block(t)
        last = t == steps - 1
        rows_up = pl.ds(0, half) if last else pl.ds(0, 2 * half)
        rows_down = pl.ds(half, half) if last else pl.ds(0, 2 * half)
        from_up = x_ref if t == 0 else out_ref.at[up]
        from_down = x_ref if t == 0 else out_ref.at[down]
        moving = (
            send(from_up.at[rows_up], out_ref.at[up, rows_up], above, up_send.at[t], up_recv.at[t]),
            send(from_down.at[rows_down], out_ref.at[down, rows_down], below, down_send.at[t], down_recv.at[t]),
        )
        sent.extend(moving)
        for copy, offset, rows in zip(moving, (-t - 1, t + 1), (rows_up, rows_down)):
            copy.wait_recv()
            here = out_ref.at[block(offset), rows]
            spot = len(pairs)
            pairs.append(send(here, here, pair, pair_send.at[spot], pair_recv.at[spot]))
    for copy in sent:
        copy.wait_send()
    for copy in pairs:
        copy.wait()
    own.wait()


def gather(x, devices, collective_id):
    chips = devices // 2
    steps = chips // 2
    dma = pltpu.SemaphoreType.DMA
    return pl.pallas_call(
        functools.partial(gather_kernel, chips),
        in_specs=[pl.BlockSpec(memory_space=pl.ANY)],
        out_specs=pl.BlockSpec(memory_space=pl.ANY),
        out_shape=jax.ShapeDtypeStruct((devices,) + x.shape, x.dtype),
        scratch_shapes=[dma] + [dma((steps,))] * 4 + [dma((2 * steps + 1,))] * 2,
        compiler_params=pltpu.CompilerParams(collective_id=collective_id, has_side_effects=True),
        cost_estimate=pl.CostEstimate(flops=0, bytes_accessed=2 * devices * x.size * x.dtype.itemsize, transcendentals=0),
    )(x)


def power_of_two(peak, most):
    ratio = jnp.where(peak > 0, peak, 1.0) / most
    return jnp.clip(jnp.ceil(jnp.log2(ratio)), -120, 120).astype(jnp.int32)


def unpack(packed):
    low = (packed << 16) >> 16
    return (packed - low) >> 16, low


def pieces(whole):
    upper = (whole + 128) >> 8
    return (upper * 256).astype(f32).astype(bf16), (whole - upper * 256).astype(f32).astype(bf16)


def steer_kernel(blocks, low_ref, high_ref, coarse_ref, fine_ref, turn_ref, out_ref, acc, rhs_t, rhs_b):
    step = pl.program_id(0)
    rows, width = low_ref.shape[1:]
    coarse = width // FINE

    row = lax.broadcasted_iota(jnp.int32, (width, width), 0)
    col = lax.broadcasted_iota(jnp.int32, (width, width), 1)
    flip = (row + col == width - 1).astype(bf16)
    low_t, low_b = halves(jnp.concatenate([low_ref[0], low_ref[1]], 0))
    low = dot1(low_t, flip) + dot1(low_b, flip)
    high = jnp.concatenate([high_ref[0], high_ref[1]], 0)
    total, diff = high + low, high - low
    left = jnp.concatenate([total, jnp.concatenate([-diff[rows:], diff[:rows]], 0)], 1)
    left_t, left_b = halves(left)

    fine_c, fine_s = fine_ref[0], fine_ref[1]
    for q in range(coarse):
        cc, cs = coarse_ref[0, q : q + 1, :], coarse_ref[1, q : q + 1, :]
        for part, value in enumerate((cc * fine_c - cs * fine_s, cs * fine_c + cc * fine_s)):
            top, rest = halves(value)
            place = pl.ds(part * width + q * FINE, FINE)
            rhs_t[place, :] = top
            rhs_b[place, :] = rest
    top = rhs_t[...]
    term = dot1(left_t, top) + dot1(left_t, rhs_b[...]) + dot1(left_b, top)

    @pl.when(step == 0)
    def _():
        acc[...] = term

    @pl.when(step > 0)
    def _():
        acc[...] += term

    @pl.when(step == blocks - 1)
    def _():
        turn_c, turn_s = turn_ref[0:1, :], turn_ref[1:2, :]
        re, im = acc[:rows, :], acc[rows:, :]
        out_ref[0] = re * turn_c - im * turn_s
        out_ref[1] = re * turn_s + im * turn_c


def steer_product(inverse, odd):
    _, rows, length = inverse.shape
    cols = odd.shape[0]
    width = min(256, length // 2)
    blocks = length // 2 // width
    half_turn = 4 * length
    coarse = jnp.stack(cis(2 * FINE * jnp.arange(length // 2 // FINE, dtype=jnp.int32)[:, None] * odd[None, :], half_turn))
    fine = jnp.stack(cis((2 * jnp.arange(FINE, dtype=jnp.int32)[:, None] + 1) * odd[None, :], half_turn))
    turn = jnp.stack(cis((length - 1) * odd, half_turn))
    return pl.pallas_call(
        functools.partial(steer_kernel, blocks),
        grid=(blocks,),
        in_specs=[
            pl.BlockSpec((2, rows, width), lambda i: (0, 0, blocks - 1 - i)),
            pl.BlockSpec((2, rows, width), lambda i: (0, 0, blocks + i)),
            pl.BlockSpec((2, width // FINE, cols), lambda i: (0, i, 0)),
            pl.BlockSpec((2, FINE, cols), lambda i: (0, 0, 0)),
            pl.BlockSpec((2, cols), lambda i: (0, 0)),
        ],
        out_specs=pl.BlockSpec((2, rows, cols), lambda i: (0, 0, 0)),
        out_shape=jax.ShapeDtypeStruct((2, rows, cols), f32),
        scratch_shapes=[
            pltpu.VMEM((2 * rows, cols), f32),
            pltpu.VMEM((2 * width, cols), bf16),
            pltpu.VMEM((2 * width, cols), bf16),
        ],
        compiler_params=pltpu.CompilerParams(vmem_limit_bytes=VMEM_LIMIT),
        cost_estimate=pl.CostEstimate(
            flops=3 * 2 * 2 * rows * length * cols, bytes_accessed=8 * rows * length, transcendentals=0
        ),
    )(inverse, inverse, coarse, fine, turn)


def definite_inverse(matrix):
    size = matrix.shape[0]
    row = lax.broadcasted_iota(jnp.int32, (size, size), 0)
    col = lax.broadcasted_iota(jnp.int32, (size, size), 1)
    eye = (row == col).astype(f32)
    scale_c = lax.rsqrt(jnp.sum(matrix * eye, axis=1, keepdims=True))
    scale_r = lax.rsqrt(jnp.sum(matrix * eye, axis=0, keepdims=True))
    unit = matrix * scale_c * scale_r
    bound = jnp.max(jnp.sum(jnp.abs(unit), axis=0, keepdims=True))
    start = eye * (1.0 / bound)
    unit_t = unit.astype(bf16)

    def square(x):
        return jnp.sum(x * x)

    def rough_next(state):
        guess, _, last, count = state
        guess_t = guess.astype(bf16)
        residual = eye - dot1(unit_t, guess_t)
        return guess + dot1(guess_t, residual.astype(bf16)), last, square(residual), count + 1

    def rough_more(state):
        _, before, last, count = state
        return (last > 0.05) & (last < before) & (count < 16)

    big = jnp.float32(1e30)
    rough = lax.while_loop(rough_more, rough_next, (start, big * 2, big, jnp.int32(0)))[0]
    first = square(eye - dot6(unit, rough))
    guess = jnp.where(first < 0.9, rough, start)

    def fine_next(state):
        guess, _, last, count = state
        residual = eye - dot6(unit, guess)
        return guess + dot6(guess, residual), last, square(residual), count + 1

    def fine_more(state):
        _, before, last, count = state
        stalled = (last < 0.25) & (last > 0.5 * before)
        return (last > 1e-6) & jnp.logical_not(stalled) & (count < 50)

    guess = lax.while_loop(fine_more, fine_next, (guess, big * 2, big, jnp.int32(0)))[0]
    return guess * scale_c * scale_r


def finish_kernel(steps, window, length, cap_ref, cross_ref, q_ref, applied_ref, fold_ref, weights_ref, spectrum_ref, work, left):
    count = 2 * steps
    snap = cap_ref.shape[1] // count
    size = 2 * snap
    rows = q_ref.shape[1]
    lead = 2 * snap
    dirs = cross_ref.shape[2]
    eye = (
        lax.broadcasted_iota(jnp.int32, (snap, snap), 0) == lax.broadcasted_iota(jnp.int32, (snap, snap), 1)
    ).astype(f32) * window
    for i in range(count):
        up, mid, down = i * size, i * size + snap, (i + 1) * size
        for j in range(count):
            at, half, end = j * size, j * size + snap, (j + 1) * size
            re = cap_ref[0, i * snap : (i + 1) * snap, j * snap : (j + 1) * snap]
            im = cap_ref[1, i * snap : (i + 1) * snap, j * snap : (j + 1) * snap]
            if i == j:
                re = re + (eye if i % 2 == 0 else -eye)
            work[up:mid, at:half] = re
            work[up:mid, half:end] = -im
            work[mid:down, at:half] = im
            work[mid:down, half:end] = re
        re = q_ref[0, :, i * snap : (i + 1) * snap]
        im = q_ref[1, :, i * snap : (i + 1) * snap]
        left[:rows, up:mid] = re
        left[:rows, mid:down] = -im
        if i < 2:
            left[rows:, up:mid] = im
            left[rows:, mid:down] = re

    def body(k, carry):
        sign = jnp.where(k % 2 == 0, 1.0, -1.0)
        here = pl.ds(pl.multiple_of(k * size, size), size)
        pivot = definite_inverse(sign * work[here, here]) * sign
        across = dot6(pivot, work[here, :])
        work[here, :] = across
        work[here, here] = pivot

        def other(step, carry):
            i = lax.rem(k + step, count)
            there = pl.ds(pl.multiple_of(i * size, size), size)
            column = work[there, here]
            work[there, here] = jnp.zeros_like(column)
            work[there, :] -= dot6(column, work[here, :])
            return carry

        lax.fori_loop(1, count, other, 0)

        @pl.when(k == 1)
        def _():
            stacked = jnp.concatenate(
                [cross_ref[p, i * snap : (i + 1) * snap] for i in range(2) for p in range(2)], 0
            )
            solved = dot3(work[: 2 * size, : 2 * size], stacked)
            drop = jnp.sum(stacked * solved, axis=0, keepdims=True)
            moved = dot3(left[:, : 2 * size], solved)
            first = cross_ref[0, lead : lead + 1]
            second = cross_ref[1, lead : lead + 1] - drop
            first, second = length / first, length / second
            spectrum_ref[0:1] = first
            spectrum_ref[1:2] = second
            for p in range(2):
                weights_ref[0, p] = applied_ref[p, :, :dirs] * first
                weights_ref[1, p] = (applied_ref[p, :, dirs:] - moved[p * rows : (p + 1) * rows]) * second

        return carry

    lax.fori_loop(0, count, body, 0)
    fold = dot3(left[:rows], work[...])
    for i in range(count):
        fold_ref[0, :, i * snap : (i + 1) * snap] = fold[:, i * size : i * size + snap]
        fold_ref[1, :, i * snap : (i + 1) * snap] = -fold[:, i * size + snap : (i + 1) * size]


def finish(cap, cross, q, applied, steps, window, length):
    order = cap.shape[1]
    rows = q.shape[1]
    dirs = cross.shape[2]
    return pl.pallas_call(
        functools.partial(finish_kernel, steps, window, length),
        in_specs=[pl.BlockSpec(memory_space=pltpu.VMEM)] * 4,
        out_specs=[pl.BlockSpec(memory_space=pltpu.VMEM)] * 3,
        out_shape=[
            jax.ShapeDtypeStruct((2, rows, order), f32),
            jax.ShapeDtypeStruct((steps, 2, rows, dirs), f32),
            jax.ShapeDtypeStruct((steps, dirs), f32),
        ],
        scratch_shapes=[pltpu.VMEM((2 * order, 2 * order), f32), pltpu.VMEM((2 * rows, 2 * order), f32)],
        compiler_params=pltpu.CompilerParams(vmem_limit_bytes=VMEM_LIMIT),
        cost_estimate=pl.CostEstimate(flops=50 * 10**9, bytes_accessed=10**7, transcendentals=0),
    )(cap, cross, q, applied)


def update_kernel(inv_ref, fold_ref, part_ref, out_ref):
    rows = inv_ref.shape[1]
    scale = jnp.exp2(part_ref[0, rows : rows + 2].astype(f32))
    fold_re = jnp.concatenate([fold_ref[0] * scale[0:1, :], fold_ref[1] * scale[1:2, :]], 1)
    fold_im = jnp.concatenate([fold_ref[1] * scale[0:1, :], -fold_ref[0] * scale[1:2, :]], 1)
    top, rest = halves(jnp.concatenate([fold_re, fold_im], 0))
    upper, lower = pieces(jnp.concatenate(unpack(part_ref[0, :rows]), 1))
    dims = ((1,), (1,))
    change = dot1(top, upper, dims) + dot1(rest, upper, dims) + dot1(top, lower, dims)
    out_ref[0] = inv_ref[0] - change[:rows]
    out_ref[1] = inv_ref[1] - change[rows:]


def low_rank_update(inverse, fold, parts_all):
    _, rows, length = inverse.shape
    order = fold.shape[2]
    return pl.pallas_call(
        update_kernel,
        grid=(length // rows,),
        in_specs=[
            pl.BlockSpec((2, rows, rows), lambda i: (0, 0, i)),
            pl.BlockSpec((2, rows, order), lambda i: (0, 0, 0)),
            pl.BlockSpec((1, rows + TAIL, order), lambda i: (i, 0, 0)),
        ],
        out_specs=pl.BlockSpec((2, rows, rows), lambda i: (0, 0, i)),
        out_shape=jax.ShapeDtypeStruct(inverse.shape, f32),
        compiler_params=pltpu.CompilerParams(vmem_limit_bytes=VMEM_LIMIT),
        cost_estimate=pl.CostEstimate(
            flops=24 * rows * order * length, bytes_accessed=16 * rows * length, transcendentals=0
        ),
    )(inverse, fold, parts_all)


def product_kernel(blocks, inv_ref, all_ref, applied_ref, coarse_ref, fine_ref, q_ref, parts_ref, acc, steer):
    step = pl.program_id(0)
    rows = inv_ref.shape[1]
    order = all_ref.shape[2]
    left = jnp.concatenate(halves(jnp.concatenate([inv_ref[0], inv_ref[1]], 0)), 0)
    right = jnp.concatenate(
        [jnp.concatenate([all_ref[i, :rows], all_ref[i, rows:]], 1) for i in range(all_ref.shape[0])], 0
    )
    term = dot1(left, right)

    @pl.when(step == 0)
    def _():
        acc[...] = term

    @pl.when(step > 0)
    def _():
        acc[...] += term

    @pl.when(step == blocks - 1)
    def _():
        total = acc[: 2 * rows] + acc[2 * rows :]
        re = total[:rows, :order] - total[rows:, order:]
        im = total[:rows, order:] + total[rows:, :order]
        q_ref[0] = re
        q_ref[1] = im
        parts_ref[rows:] = jnp.zeros((TAIL, order), jnp.int32)
        packed = 0
        for part, value in enumerate((re, im)):
            power = power_of_two(jnp.max(jnp.abs(value), axis=0, keepdims=True), 32767.0)
            parts_ref[rows + part : rows + part + 1] = power
            whole = jnp.round(value / jnp.exp2(power.astype(f32)))
            packed = packed * 65536 + jnp.clip(whole, -32767, 32767).astype(jnp.int32)
        parts_ref[:rows] = packed

        cols = steer.shape[2]
        dirs = cols // 2
        fine_c, fine_s = fine_ref[0], fine_ref[1]
        for g in range(rows // FINE):
            cc, cs = coarse_ref[0, g : g + 1, :], coarse_ref[1, g : g + 1, :]
            steer[0, g * FINE : (g + 1) * FINE, :] = cc * fine_c - cs * fine_s
            steer[1, g * FINE : (g + 1) * FINE, :] = cs * fine_c + cc * fine_s
        sums = jnp.sum(steer[0] * applied_ref[0] + steer[1] * applied_ref[1], axis=0, keepdims=True)
        power = power_of_two(jnp.max(jnp.abs(sums), axis=1, keepdims=True), 2.0**30)
        whole = jnp.round(sums / jnp.exp2(power.astype(f32))).astype(jnp.int32)
        parts_ref[rows + 2 : rows + 3, :dirs] = whole[:, :dirs]
        parts_ref[rows + 3 : rows + 4, :dirs] = whole[:, dirs:]
        parts_ref[rows + 4 : rows + 5, :dirs] = jnp.broadcast_to(power, (1, dirs))


def product(inverse, snaps_all, applied, coarse, fine):
    _, rows, length = inverse.shape
    order = snaps_all.shape[2]
    cols = applied.shape[2]
    group = 2
    blocks = length // rows // group
    keep = lambda *shape: pl.BlockSpec(shape, lambda i: (0,) * len(shape))
    shapes = [((2, rows, order), f32), ((rows + TAIL, order), jnp.int32)]
    return pl.pallas_call(
        functools.partial(product_kernel, blocks),
        grid=(blocks,),
        in_specs=[
            pl.BlockSpec((2, rows, group * rows), lambda i: (0, 0, i)),
            pl.BlockSpec((group, 2 * rows, order), lambda i: (i, 0, 0)),
            keep(*applied.shape),
            keep(*coarse.shape),
            keep(*fine.shape),
        ],
        out_specs=[keep(*shape) for shape, _ in shapes],
        out_shape=[jax.ShapeDtypeStruct(shape, kind) for shape, kind in shapes],
        scratch_shapes=[pltpu.VMEM((4 * rows, 2 * order), f32), pltpu.VMEM((2, rows, cols), f32)],
        compiler_params=pltpu.CompilerParams(vmem_limit_bytes=VMEM_LIMIT),
        cost_estimate=pl.CostEstimate(
            flops=16 * rows * length * order, bytes_accessed=16 * rows * length, transcendentals=0
        ),
    )(inverse, snaps_all, applied, coarse, fine)


def sums_kernel(blocks, parts_ref, snaps_ref, cap_ref, power_ref, acc, powers):
    step = pl.program_id(0)
    rows = snaps_ref.shape[1] // 2
    order = snaps_ref.shape[2]
    dirs = power_ref.shape[2]

    @pl.when(step == 0)
    def _():
        acc[...] = jnp.zeros_like(acc)
        powers[...] = jnp.zeros_like(powers)

    dims = ((0,), (0,))
    re, im = unpack(parts_ref[0, :rows])
    scales = jnp.exp2(parts_ref[0, rows : rows + 2].astype(f32))
    snaps = jnp.concatenate([snaps_ref[0, :rows], snaps_ref[0, rows:]], 1)
    upper, lower = pieces(jnp.concatenate([re, im], 1))
    scale = jnp.concatenate([scales[0:1], scales[1:2]], 1)
    acc[...] += (dot1(snaps, upper, dims) + dot1(snaps, lower, dims)) * scale

    unit = jnp.exp2(parts_ref[0, rows + 4 : rows + 5, :dirs].astype(f32))
    powers[0:1] += parts_ref[0, rows + 2 : rows + 3, :dirs].astype(f32) * unit
    powers[1:2] += parts_ref[0, rows + 3 : rows + 4, :dirs].astype(f32) * unit

    @pl.when(step == blocks - 1)
    def _():
        cap_ref[0] = acc[:order, :order] + acc[order:, order:]
        cap_ref[1] = acc[:order, order:] - acc[order:, :order]
        power_ref[0] = jnp.broadcast_to(powers[0:1], (8, dirs))
        power_ref[1] = jnp.broadcast_to(powers[1:2], (8, dirs))


def sums(parts_all, snaps_all, dirs):
    blocks, packed, order = parts_all.shape
    rows = packed - TAIL
    keep = lambda *shape: pl.BlockSpec(shape, lambda i: (0,) * len(shape))
    shapes = [(2, order, order), (2, 8, dirs)]
    return pl.pallas_call(
        functools.partial(sums_kernel, blocks),
        grid=(blocks,),
        in_specs=[
            pl.BlockSpec((1, packed, order), lambda i: (i, 0, 0)),
            pl.BlockSpec((1, 2 * rows, order), lambda i: (i, 0, 0)),
        ],
        out_specs=[keep(*shape) for shape in shapes],
        out_shape=[jax.ShapeDtypeStruct(shape, f32) for shape in shapes],
        scratch_shapes=[
            pltpu.VMEM((2 * order, 2 * order), f32),
            pltpu.VMEM((8, dirs), f32),
        ],
        compiler_params=pltpu.CompilerParams(vmem_limit_bytes=VMEM_LIMIT),
    )(parts_all, snaps_all)


def on_device(inverse, cycle, arrivals, departing, directions):
    _, rows, length = inverse.shape
    window = cycle.shape[2]
    steps, _, _, snap = arrivals.shape
    dirs = directions.shape[1]

    slots = lax.broadcasted_iota(jnp.int32, (window, steps * snap), 0)
    pick = (slots == departing.reshape(1, -1)).astype(bf16)
    departed = dot1(cycle.reshape(2 * rows, window), pick).astype(bf16).reshape(2, rows, steps, snap)
    snaps = jnp.concatenate([jnp.moveaxis(arrivals, 0, 2), departed], axis=3).reshape(2 * rows, 2 * steps * snap)
    devices = length // rows
    snaps_all = gather(snaps, devices, 0)

    odd = (2 * directions + 1 - 2 * length).reshape(-1)
    applied = steer_product(inverse, odd)

    coarse = jnp.stack(cis(FINE * jnp.arange(length // FINE, dtype=jnp.int32)[:, None] * odd[None, :], 2 * length))
    fine = jnp.stack(cis(jnp.arange(FINE, dtype=jnp.int32)[:, None] * odd[None, :], 2 * length))
    first = lax.axis_index("row") * (rows // FINE)
    local = lax.dynamic_slice_in_dim(coarse, first, rows // FINE, 1)
    q, parts = product(inverse, snaps_all, applied, local, fine)
    parts_all = gather(parts, devices, 1)
    cap, power = sums(parts_all, snaps_all, dirs)

    lead = 2 * snap
    scales = jnp.exp2(parts_all[:, rows : rows + 2, :lead].astype(f32))
    parts_re, parts_im = unpack(parts_all[:, :rows, :lead])
    block = jnp.concatenate(
        [parts_re.astype(f32) * scales[:, 0:1], parts_im.astype(f32) * scales[:, 1:2]], axis=2
    ).reshape(length, 2 * lead)
    big, small = coarse[:, :, None, dirs:], fine[:, None, :, dirs:]
    steer = jnp.concatenate(
        [big[0] * small[0] - big[1] * small[1], big[1] * small[0] + big[0] * small[1]], axis=2
    ).reshape(length, 2 * dirs)
    wide = lax.dot_general(
        block, steer, (((0,), (0,)), ((), ())), precision=lax.Precision.HIGH, preferred_element_type=f32
    )
    cross = jnp.stack([
        wide[:lead, :dirs] + wide[lead:, dirs:],
        wide[:lead, dirs:] - wide[lead:, :dirs],
    ])
    cross = jnp.concatenate([cross, power], axis=1)

    fold, weights, spectrum = finish(cap, cross, q, applied, steps, window, length)
    new_inverse = low_rank_update(inverse, fold, parts_all)
    return new_inverse, weights, spectrum


def solution(mesh):
    in_specs = (
        P("groups", "row", None),
        P("groups", "row", None),
        P("groups", None, "row", None),
        P("groups", None),
        P("groups", None),
    )
    out_specs = (P("groups", "row", None), P("groups", None, "row", None), P("groups", None))
    return jax.shard_map(
        on_device, mesh=mesh, in_specs=in_specs, out_specs=out_specs, check_vma=False
    )
```
